32 devices in a mesh: parts: 2 (over y), req: 4 (over z), tp: 4 (over x, core).
Axes of the slice: x: 2, y: 2, z: 4, core: 2. Of those that a mesh axis runs over, the one named last changes fastest.
Arguments:
- prompts: bfloat16 [8192, 8192], P(('parts', 'req'), 'tp'), parts along dimension 0, may hold values from -6 to 6
- kv_weight: bfloat16 [8192, 2048], P('tp', 'req'), may hold values from -0.0625 to 0.0625
- owners: int32 [8, 4], P(('parts', 'req')), parts along dimension 0, may hold values from 0 to 3, as said below
- pages: int32 [8, 4], P(('parts', 'req')), parts along dimension 0, may hold values from 1 to 40, as said below
- lengths: int32 [8, 4], P(('parts', 'req')), parts along dimension 0, may hold values from 1 to 640, as said below
- queries: bfloat16 [2, 32, 8192], P(None, ('parts', 'req'), 'tp'), parts along dimension 1, may hold values from -100 to 100
- new_kv: bfloat16 [2, 32, 2048], P(None, ('parts', 'req'), 'tp'), parts along dimension 1, may hold values from -100 to 100
Outputs:
- attended: bfloat16 [2, 32, 8192], P(None, ('parts', 'req'), 'tp'), parts along dimension 1
The draws below stay inside these ranges and needn't reach their ends.
There are 2 independent parts, one for each index of `parts`. The reference program is written for one: setup_inputs(seed, part) draws one part's arguments, and reference() takes and returns one part's arrays. A program takes and returns all parts, laid end to end along the dimension named above; an argument that names none is the same for every part. Nothing has to cross between parts.
Inputs may be any that keep to these rules, and one draw needn't show every extreme that they name: Each row of owners names every decode owner once. Each row sums to 64; in each row one request has exactly 40 pages. lengths[o, g] is the token count of the request of group g served by owner o: more than 16 * (its pages - 1) and at most 16 * its pages.
All inputs are finite; a program needn't handle non-finite values.
Results may differ from the reference program's by a relative error of at most 0.017.
Values may be sent and summed in bfloat16 or wider, within the bound.
A program may use at most 64 MiB of HBM per device.

```python
import jax
import jax.numpy as jnp
from jax import lax

D = 8192
QH = 64
KVH = 8
HD = 128
PAGE = 16
STEPS = 2
TOK_PREF = 1024
GQA = 8
KV_COLS = 2048
GROUP_PAGES = 64
MOST_PAGES = 40
PROMPTS = 4096
ROWS = 16
N_REQ = 4
N_TP = 4


def request_plan(key):
    places = jnp.arange(N_REQ, dtype=jnp.int32)

    def one_group(group):
        group_key = jax.random.fold_in(key, group)
        owner_row = jax.random.permutation(jax.random.fold_in(group_key, 1), N_REQ).astype(jnp.int32)
        largest = jax.random.randint(jax.random.fold_in(group_key, 2), (), 0, N_REQ)
        counts = jnp.where(places == largest, MOST_PAGES, 1).astype(jnp.int32)

        def add_page(turn_index, current):
            scores = jax.random.randint(jax.random.fold_in(group_key, 100 + turn_index), (N_REQ,), 0, 1 << 20) * N_REQ + places
            allowed = (current < MOST_PAGES) & (places != largest)
            picked = jnp.argmax(jnp.where(allowed, scores, -1))
            return current + (places == picked).astype(jnp.int32)
        counts = lax.fori_loop(0, GROUP_PAGES - MOST_PAGES - (N_REQ - 1), add_page, counts)
        trimmed = jnp.where(places == largest, 0, jax.random.randint(jax.random.fold_in(group_key, 3), (N_REQ,), 0, PAGE))
        return (owner_row, counts, counts * PAGE - trimmed)
    owner_table, page_table, token_lengths = jax.vmap(one_group)(places)
    matches = (owner_table[:, :, None] == places[None, None, :]).astype(jnp.int32)
    by_group = jnp.sum(token_lengths[:, :, None] * matches, axis=1)
    return (owner_table, page_table, by_group.T)


def decode_draw(key, strength):
    fresh = jax.random.normal(jax.random.fold_in(key, 11), (STEPS, ROWS, KVH, 2, HD), jnp.float32)
    asked = jax.random.normal(jax.random.fold_in(key, 12), (STEPS, ROWS, KVH, GQA, HD), jnp.float32)
    chosen = (jax.random.randint(jax.random.fold_in(key, 13), (ROWS,), 0, 8) == 0).astype(jnp.float32) * strength
    select = chosen[:, None, None]
    second = (1.0 - select) * fresh[1, :, :, 0]
    fresh = fresh.at[1, :, :, 0].set(second)
    pick = chosen[None, :, None, None, None]
    asked = (1.0 - pick) * asked
    asked = jnp.clip(asked, -100.0, 100.0)
    return (asked.reshape(STEPS, ROWS, QH * HD), fresh.reshape(STEPS, ROWS, KV_COLS))


def draw_owners(key, part):
    return request_plan(key)[0]


def draw_pages(key, part):
    return request_plan(key)[1]


def draw_lengths(key, part):
    return request_plan(key)[2]


def draw_queries(key, part):
    drawn = decode_draw(key, 0.0)
    return drawn[0].astype(jnp.bfloat16)


def draw_new_kv(key, part):
    drawn = decode_draw(key, 0.0)
    return drawn[1].astype(jnp.bfloat16)


def level_of(own_key, shape, shards, low, high):
    gain, own = 1.0, jax.random.fold_in(own_key, 6)
    for axis_at, shards_of in shards:
        draws = jnp.exp(jax.random.uniform(jax.random.fold_in(own, axis_at), (shards_of,), jnp.float32, low / len(shards), high / len(shards)))
        gain = gain * jnp.repeat(draws, shape[axis_at] // shards_of).reshape([-1 if axis == axis_at else 1 for axis in range(len(shape))])
    return gain


def noise(own_key, shape, deviation, reach, split=(), kind=jnp.bfloat16):
    array = deviation * jax.random.normal(own_key, shape, jnp.float32)
    if split:
        array = array * level_of(own_key, shape, split, -0.22, 0.18)
    return jnp.clip(array, -reach, reach).astype(kind)


def setup_inputs(seed: int = 0, part: int = 0) -> dict:
    seeds = jax.random.split(jax.random.key(seed), 8)
    part_keys = jax.random.split(jax.random.fold_in(seeds[7], part), 8)
    prompts = noise(part_keys[0], (PROMPTS, D), 1.0, 6.0, ((0, 4), (1, 4)))
    kv_weight = noise(seeds[1], (D, KV_COLS), D ** -0.5, 0.0625, ((0, 4), (1, 4)))
    owners = draw_owners(jax.random.fold_in(jax.random.fold_in(seeds[7], part), 71), part)
    pages = draw_pages(jax.random.fold_in(jax.random.fold_in(seeds[7], part), 71), part)
    lengths = draw_lengths(jax.random.fold_in(jax.random.fold_in(seeds[7], part), 71), part)
    queries = draw_queries(jax.random.fold_in(jax.random.fold_in(seeds[7], part), 71), part)
    new_kv = draw_new_kv(jax.random.fold_in(jax.random.fold_in(seeds[7], part), 71), part)
    return dict(prompts=prompts, kv_weight=kv_weight, owners=owners, pages=pages, lengths=lengths, queries=queries, new_kv=new_kv)


def project_group(span, kv_weight):
    block_width = D // N_TP
    summed = jnp.zeros((span.shape[0], kv_weight.shape[1]), jnp.float32)
    for block in range(N_TP):
        partial_value = jnp.dot(span[:, block * block_width:(block + 1) * block_width], kv_weight[block * block_width:(block + 1) * block_width], preferred_element_type=jnp.float32)
        rounded = lax.optimization_barrier(partial_value.astype(jnp.bfloat16))
        summed = summed + rounded.astype(jnp.float32)
    return summed.astype(jnp.bfloat16)


def slice_requests(key_value, page_row):
    slot_tokens = MOST_PAGES * PAGE
    padded = jnp.concatenate([key_value, jnp.zeros((slot_tokens, key_value.shape[1]), key_value.dtype)], axis=0)
    starts = ((jnp.cumsum(page_row) - page_row) * PAGE).astype(jnp.int32)
    return jax.vmap(lambda offset: lax.dynamic_slice_in_dim(padded, offset, slot_tokens, 0))(starts)


def attend(queries, new_kv, cache, row_lengths):
    steps_count, rows_count = queries.shape[0], queries.shape[1]
    heads_kv = new_kv.shape[2] // (2 * HD)
    slot_tokens = cache.shape[1]
    score_scale = HD ** -0.5
    asked = queries.reshape(steps_count, rows_count, heads_kv, GQA, HD).astype(jnp.float32)
    fresh = new_kv.reshape(steps_count, rows_count, heads_kv, 2, HD).astype(jnp.float32)
    stored = cache.reshape(rows_count, slot_tokens, heads_kv, 2, HD)
    cached_keys = stored[:, :, :, 0].astype(jnp.float32)
    cached_values = stored[:, :, :, 1].astype(jnp.float32)
    cached = jnp.einsum("srhgd,rthd->srhgt", asked, cached_keys) * score_scale
    newer = jnp.einsum("srhgd,urhd->srhgu", asked, fresh[:, :, :, 0]) * score_scale
    valid = jnp.arange(slot_tokens, dtype=jnp.int32)[None, :] < row_lengths[:, None]
    seen = jnp.arange(steps_count)[None, :] <= jnp.arange(steps_count)[:, None]
    cached = jnp.where(valid[None, :, None, None, :], cached, -1e30)
    newer = jnp.where(seen[:, None, None, None, :], newer, -1e30)
    top = jnp.maximum(jnp.max(cached, axis=-1), jnp.max(newer, axis=-1))[..., None]
    weight_cached = jnp.exp(cached - top)
    weight_newer = jnp.exp(newer - top)
    total = jnp.sum(weight_cached, axis=-1, keepdims=True) + jnp.sum(weight_newer, axis=-1, keepdims=True)
    prob_cached = (weight_cached / total).astype(jnp.bfloat16)
    prob_newer = (weight_newer / total).astype(jnp.bfloat16)
    mixed = jnp.einsum("srhgt,rthd->srhgd", prob_cached.astype(jnp.float32), cached_values)
    mixed = mixed + jnp.einsum("srhgu,urhd->srhgd", prob_newer.astype(jnp.float32), fresh[:, :, :, 1])
    return mixed.astype(jnp.bfloat16).reshape(steps_count, rows_count, heads_kv * GQA * HD)


def reference(prompts, kv_weight, owners, pages, lengths, queries, new_kv):
    spans = prompts.reshape(N_REQ, TOK_PREF, D)

    def per_group(items):
        span, page_row = items
        return slice_requests(project_group(span, kv_weight), page_row)

    slices = lax.map(per_group, (spans, pages))
    slot_tokens = MOST_PAGES * PAGE
    row_index = (owners * N_REQ + jnp.arange(N_REQ, dtype=jnp.int32)[:, None]).astype(jnp.int32)
    cache = jnp.zeros((ROWS, slot_tokens, KV_COLS), jnp.bfloat16)
    cache = cache.at[row_index.reshape(-1)].set(slices.reshape(N_REQ * N_REQ, slot_tokens, KV_COLS))
    return attend(queries, new_kv, cache, lengths.reshape(-1).astype(jnp.int32))
```

```python
import functools

import jax
import jax.numpy as jnp
from jax import lax
from jax.experimental import pallas as pl
from jax.experimental.pallas import tpu as pltpu
from jax.sharding import PartitionSpec as P

HD = 128
PAGE = 16
GQA = 8
CHUNKS = 2
TILE = 256
MESH = pl.DeviceIdType.MESH
SCALE = HD ** (-0.5)


def attend(queries, new_kv, cache, row_lengths):
    steps_count, rows_count = (queries.shape[0], queries.shape[1])
    heads_kv = new_kv.shape[2] // (2 * HD)
    slot_tokens = cache.shape[1]
    score_scale = HD ** (-0.5)
    asked = queries.reshape(steps_count, rows_count, heads_kv, GQA, HD)
    fresh = new_kv.reshape(steps_count, rows_count, heads_kv, 2, HD)
    stored = cache.reshape(rows_count, slot_tokens, heads_kv, 2, HD)
    cached = (
        jnp.einsum(
            "srhgd,rthd->srhgt", asked, stored[:, :, :, 0], preferred_element_type=jnp.float32
        )
        * score_scale
    )
    newer = (
        jnp.einsum(
            "srhgd,urhd->srhgu", asked, fresh[:, :, :, 0], preferred_element_type=jnp.float32
        )
        * score_scale
    )
    valid = jnp.arange(slot_tokens, dtype=jnp.int32)[None, :] < row_lengths[:, None]
    seen = jnp.arange(steps_count)[None, :] <= jnp.arange(steps_count)[:, None]
    cached = jnp.where(valid[None, :, None, None, :], cached, -1e30)
    newer = jnp.where(seen[:, None, None, None, :], newer, -1e30)
    top = jnp.maximum(jnp.max(cached, axis=-1), jnp.max(newer, axis=-1))[..., None]
    weight_cached = jnp.exp(cached - top)
    weight_newer = jnp.exp(newer - top)
    total = jnp.sum(weight_cached, axis=-1, keepdims=True) + jnp.sum(
        weight_newer, axis=-1, keepdims=True
    )
    prob_cached = (weight_cached / total).astype(jnp.bfloat16)
    prob_newer = (weight_newer / total).astype(jnp.bfloat16)
    mixed = jnp.einsum(
        "srhgt,rthd->srhgd", prob_cached, stored[:, :, :, 1], preferred_element_type=jnp.float32
    )
    mixed = mixed + jnp.einsum(
        "srhgu,urhd->srhgd", prob_newer, fresh[:, :, :, 1], preferred_element_type=jnp.float32
    )
    return mixed.astype(jnp.bfloat16).reshape(steps_count, rows_count, heads_kv * GQA * HD)


def general(prompts, kv_weight, owners, pages, lengths, queries, new_kv):
    owner_count = lax.axis_size("req")
    tokens_here = prompts.shape[0]
    group_pages = tokens_here // PAGE
    most_pages = 5 * group_pages // (2 * owner_count)
    slot_tokens = most_pages * PAGE
    partial_value = jnp.dot(
        prompts,
        lax.all_gather(kv_weight, "req", axis=1, tiled=True),
        preferred_element_type=jnp.float32,
    )
    key_value = lax.psum_scatter(
        partial_value.astype(jnp.bfloat16), "tp", scatter_dimension=1, tiled=True
    )
    width_here = key_value.shape[1]
    padded = jnp.concatenate(
        [key_value, jnp.zeros((slot_tokens, width_here), jnp.bfloat16)], axis=0
    )
    starts = jnp.cumsum(pages[0]) - pages[0]
    chosen_mask = (owners[0][None, :] == jnp.arange(owner_count, dtype=jnp.int32)[:, None]).astype(
        jnp.int32
    )
    target_starts = jnp.sum(chosen_mask * starts[None, :], axis=1) * PAGE
    outgoing = jax.vmap(lambda offset: lax.dynamic_slice_in_dim(padded, offset, slot_tokens, 0))(
        target_starts
    )
    incoming = lax.all_to_all(outgoing, "req", split_axis=0, concat_axis=0, tiled=True)
    return attend(queries, new_kv, incoming, lengths[0])


def kernel(
    R, T, owners, pages, lengths, x_hbm, w_hbm, small, out,
    x, w, kvb, msg, qall, lens_out, lens_in, tok, s_part, s_recv, p_all, fresh_o,
    o_part, o_recv, o_send, fin,
    x_sem, w_sem, msg_s, msg_r, len_s, len_r, q_s, q_r,
    z_s, z_r, y_s, y_r, s_s, s_r, p_s, p_r, o_s, o_r, f_s, f_r,
):
    p, r, t = lax.axis_index("parts"), lax.axis_index("req"), lax.axis_index("tp")
    tokens = x.shape[0]
    features = w.shape[2]
    part_rows = features // CHUNKS
    ht = small.shape[1]
    heads = R * 2
    rows = small.shape[3]
    f32 = jnp.float32

    def when(cond):
        return pl.when(cond)

    x_copy = pltpu.make_async_copy(x_hbm, x, x_sem)
    own = [
        pltpu.make_async_copy(
            w_hbm.at[:, pl.ds((2 * i + kv) * HD, HD)], w.at[kv, 2 * r + i], w_sem.at[kv, i]
        )
        for kv in range(2)
        for i in range(2)
    ]
    for copy in own:
        copy.start()
    x_copy.start()

    barrier = pltpu.get_barrier_semaphore()
    for rel in range(1, R):
        pl.semaphore_signal(barrier, inc=1, device_id={"req": lax.rem(r + rel, R)}, device_id_type=MESH)
    for rel in range(1, T):
        pl.semaphore_signal(barrier, inc=1, device_id={"tp": lax.rem(t + rel, T)}, device_id_type=MESH)
    pl.semaphore_signal(barrier, inc=1, device_id={"parts": 1 - p}, device_id_type=MESH)

    lane = lax.broadcasted_iota(jnp.int32, (8, 128), 1)
    row_len = jnp.zeros((8, 128), jnp.int32)
    for g in range(R):
        row_len = jnp.where(lane == g, lengths[0, g], row_len)
    lens_out[...] = row_len
    lens_in[r] = row_len
    msg[r] = small[r]

    for copy in own:
        copy.wait()
    pl.semaphore_wait(barrier, R + T - 1)

    def remote(src, dst, s, d, where):
        return pltpu.make_async_remote_copy(
            src_ref=src, dst_ref=dst, send_sem=s, recv_sem=d, device_id=where, device_id_type=MESH
        )

    def msg_copy(rel):
        to = lax.rem(r + rel, R)
        return remote(small.at[to], msg.at[r], msg_s.at[rel], msg_r.at[rel], {"req": to})

    def msg_arrival(rel):
        of = lax.rem(r + R - rel, R)
        return remote(small.at[of], msg.at[of], msg_s.at[rel], msg_r.at[rel], {"req": of})

    def len_copy(rel):
        to = lax.rem(r + rel, R)
        return remote(lens_out, lens_in.at[r], len_s.at[rel], len_r.at[rel], {"req": to})

    def len_arrival(rel):
        of = lax.rem(r + R - rel, R)
        return remote(lens_out, lens_in.at[of], len_s.at[rel], len_r.at[rel], {"req": of})

    for rel in range(1, R):
        msg_copy(rel).start()
        len_copy(rel).start()

    def piece(kv, h, c):
        return w.at[kv, h, pl.ds(pl.multiple_of(c * part_rows, part_rows), part_rows)]

    def z_copy(kv, s, c, direction):
        to = r - 1 if direction == 0 else r + 1
        ref = piece(kv, 2 * s + p, c)
        return remote(ref, ref, z_s.at[kv, s, direction, c], z_r.at[kv, s, c], {"req": to})

    def y_copy(kv, s, c):
        ref = piece(kv, 2 * s + p, c)
        return remote(ref, ref, y_s.at[kv, s, c], y_r.at[kv, s, c], {"parts": 1 - p})

    def y_arrival(kv, s, c):
        ref = piece(kv, 2 * s + 1 - p, c)
        return remote(ref, ref, y_s.at[kv, s, c], y_r.at[kv, s, c], {"parts": 1 - p})

    def z_arrival(kv, s, c, direction):
        ref = piece(kv, 2 * s + p, c)
        of = r + 1 if direction == 0 else r - 1
        return remote(ref, ref, z_s.at[kv, s, direction, c], z_r.at[kv, s, c], {"req": of})

    can = (r > 0, r < R - 1)

    def send_own(kv):
        for c in range(CHUNKS):
            for direction in range(2):
                @when(can[direction])
                def _():
                    z_copy(kv, r, c, direction).start()

    send_own(0)

    for rel in range(1, R):
        msg_arrival(rel).wait_recv()
        len_arrival(rel).wait_recv()
    for i in range(ht):
        for o in range(R):
            qall[t * ht + i, o] = msg[o, i, 0]

    def q_copy(rel):
        ref = qall.at[pl.ds(t * ht, ht)]
        return remote(ref, ref, q_s.at[rel], q_r.at[rel], {"tp": lax.rem(t + rel, T)})

    def q_arrival(rel):
        of = lax.rem(t + T - rel, T)
        ref = qall.at[pl.ds(of * ht, ht)]
        return remote(ref, ref, q_s.at[rel], q_r.at[rel], {"tp": of})

    for rel in range(1, T):
        q_copy(rel).start()

    position = lax.broadcasted_iota(jnp.int32, (rows, tokens), 1)
    owner_of = jnp.full((rows, tokens), -1, jnp.int32)
    for o in range(R):
        begin = jnp.int32(0)
        running = jnp.int32(0)
        for j in range(R):
            begin = begin + jnp.where(owners[0, j] == o, running, 0)
            running = running + pages[0, j] * PAGE
        length = jnp.sum(jnp.where(lane[:1] == r, lens_in[o][:1], 0), axis=1, keepdims=True)
        inside = (position >= begin) & (position < begin + length)
        owner_of = jnp.where(inside, o, owner_of)
    tok[...] = owner_of

    x_copy.wait()
    for rel in range(1, T):
        q_arrival(rel).wait_recv()

    def s_copy(h):
        to, i = h // ht, lax.rem(h, ht)
        return remote(s_part.at[h], s_recv.at[t, i], s_s.at[h], s_r.at[t, i], {"tp": to})

    def o_copy(h):
        to, i = h // ht, lax.rem(h, ht)
        return remote(o_part.at[h], o_recv.at[t, i], o_s.at[h], o_r.at[t, i], {"tp": to})

    def process(kv, h):
        slot = jnp.where(kv == 1, h, heads)

        def tile(n, carry):
            at = pl.ds(pl.multiple_of(n * TILE, TILE), TILE)
            kvb[slot, at, :] = jnp.dot(
                x[at, :], w[kv, h], preferred_element_type=f32
            ).astype(jnp.bfloat16)
            return carry

        lax.fori_loop(0, tokens // TILE, tile, 0)

        @when(kv == 0)
        def _():
            scores = lax.dot_general(
                qall[h].reshape(R * rows, HD), kvb[heads],
                (((1,), (1,)), ((), ())), preferred_element_type=f32,
            )
            belongs = tok[...]
            chosen = jnp.zeros((rows, tokens), f32)
            for o in range(R):
                chosen = jnp.where(belongs == o, scores[o * rows:(o + 1) * rows], chosen)
            s_part[h] = chosen

            @when(h // ht != t)
            def _():
                s_copy(h).start()

    def own_body(j, carry):
        process(j // 2, 2 * r + lax.rem(j, 2))
        return carry

    lax.fori_loop(0, 4, own_body, 0)

    def others(n):
        return [lax.rem(t + rel, n) for rel in range(1, n)]

    def p_copy(rel):
        ref = p_all.at[pl.ds(t * ht, ht)]
        return remote(ref, ref, p_s.at[rel], p_r.at[rel], {"tp": lax.rem(t + rel, T)})

    def p_arrival(rel):
        of = lax.rem(t + T - rel, T)
        ref = p_all.at[pl.ds(of * ht, ht)]
        return remote(ref, ref, p_s.at[rel], p_r.at[rel], {"tp": of})

    def softmax():
        belongs = tok[...]
        row = lax.broadcasted_iota(jnp.int32, (rows, rows), 0)
        col = lax.broadcasted_iota(jnp.int32, (rows, rows), 1)
        seen = col * GQA <= row
        for i in range(ht):
            h = t * ht + i
            total = s_part[h]
            for of in others(T):
                remote(s_part.at[h], s_recv.at[of, i], s_s.at[h], s_r.at[of, i], {"tp": of}).wait_recv()
                total = total + s_recv[of, i]
            total = total * SCALE
            probs = jnp.zeros((rows, tokens), f32)
            for o in range(R):
                newer = lax.dot_general(
                    msg[o, i, 0], msg[o, i, 1], (((1,), (1,)), ((), ())),
                    preferred_element_type=f32,
                ) * SCALE
                newer = jnp.where(seen, newer, -1e30)
                mine = jnp.where(belongs == o, total, -1e30)
                top = jnp.maximum(
                    jnp.max(mine, axis=1, keepdims=True), jnp.max(newer, axis=1, keepdims=True)
                )
                e_old = jnp.exp(mine - top)
                e_new = jnp.exp(newer - top)
                den = jnp.sum(e_old, axis=1, keepdims=True) + jnp.sum(e_new, axis=1, keepdims=True)
                probs = jnp.where(belongs == o, e_old / den, probs)
                fresh_o[i, o] = jnp.dot(
                    (e_new / den).astype(jnp.bfloat16), msg[o, i, 2], preferred_element_type=f32
                )
            p_all[h] = probs.astype(jnp.bfloat16)
        for rel in range(1, T):
            p_copy(rel).start()

    hops = R - 1
    last = 2 * hops

    def source(step, side):
        kv, d = step // hops, lax.rem(step, hops) + 1
        s = r + d if side == 0 else r - d
        valid = s < R if side == 0 else s >= 0
        return kv, s, valid

    def step_body(step, carry):
        @when(step < last)
        def _():
            for c in range(CHUNKS):
                for side in range(2):
                    kv, s, valid = source(step, side)

                    @when(valid)
                    def _():
                        z_arrival(kv, s, c, side).wait_recv()

                        @when(can[side])
                        def _():
                            z_copy(kv, s, c, side).start()

                        y_copy(kv, s, c).start()

        @when(step == 0)
        def _():
            send_own(1)

        @when(step == R)
        def _():
            softmax()

        def candidate(j, carry):
            late, side = j // 2, lax.rem(j, 2)
            at = step - late
            kv, d = jnp.maximum(at, 0) // hops, lax.rem(jnp.maximum(at, 0), hops) + 1
            s = jnp.where(side == 0, r + d, r - d)
            valid = (s < R) & (s >= 0) & (at >= 0) & (at < last)

            @when(valid)
            def _():
                @when(late == 1)
                def _():
                    for c in range(CHUNKS):
                        y_arrival(kv, s, c).wait_recv()

                process(kv, 2 * s + jnp.where(late == 1, 1 - p, p))

            return carry

        lax.fori_loop(0, 4, candidate, 0)
        return carry

    lax.fori_loop(0, last + 1, step_body, 0)

    for rel in range(1, T):
        p_arrival(rel).wait_recv()

    def mix(n, carry):
        h = lax.rem(n + t * ht + ht, heads)
        belongs = tok[...]
        probs = p_all[h].astype(f32)
        split = jnp.concatenate(
            [jnp.where(belongs == o, probs, 0.0).astype(jnp.bfloat16) for o in range(R)], axis=0
        )
        o_part[h] = jnp.dot(split, kvb[h], preferred_element_type=f32)

        @when(h // ht != t)
        def _():
            o_copy(h).start()

        return carry

    lax.fori_loop(0, heads, mix, 0)

    for i in range(ht):
        h = t * ht + i
        total = o_part[h]
        for of in others(T):
            remote(o_part.at[h], o_recv.at[of, i], o_s.at[h], o_r.at[of, i], {"tp": of}).wait_recv()
            total = total + o_recv[of, i]
        for o in range(R):
            o_send[o, i] = (total[o * rows:(o + 1) * rows] + fresh_o[i, o]).astype(jnp.bfloat16)

    def f_copy(rel):
        to = lax.rem(r + rel, R)
        return remote(o_send.at[to], fin.at[r], f_s.at[rel], f_r.at[rel], {"req": to})

    def f_arrival(rel):
        of = lax.rem(r + R - rel, R)
        return remote(o_send.at[of], fin.at[of], f_s.at[rel], f_r.at[rel], {"req": of})

    for rel in range(1, R):
        f_copy(rel).start()
    fin[r] = o_send[r]

    for rel in range(1, R):
        msg_copy(rel).wait_send()
        len_copy(rel).wait_send()
    for rel in range(1, T):
        q_copy(rel).wait_send()
        p_copy(rel).wait_send()
    for kv in range(2):
        for s in range(R):
            for c in range(CHUNKS):
                @when((s >= r) & can[0])
                def _():
                    z_copy(kv, s, c, 0).wait_send()

                @when((s <= r) & can[1])
                def _():
                    z_copy(kv, s, c, 1).wait_send()

                @when(s != r)
                def _():
                    y_copy(kv, s, c).wait_send()
    for h in range(heads):
        @when(h // ht != t)
        def _():
            s_copy(h).wait_send()
            o_copy(h).wait_send()
    for rel in range(1, R):
        f_copy(rel).wait_send()
        f_arrival(rel).wait_recv()
    out[...] = fin[...]


def fused(R, T, prompts, kv_weight, owners, pages, lengths, queries, new_kv):
    steps, count, width = queries.shape
    ht = width // (GQA * HD)
    heads = 2 * R
    rows = steps * GQA
    tokens, features = prompts.shape
    bf16, f32, i32 = jnp.bfloat16, jnp.float32, jnp.int32
    asked = queries.reshape(steps, count, ht, GQA, HD).transpose(1, 2, 0, 3, 4)
    asked = asked.reshape(count, ht, 1, rows, HD)
    fresh = new_kv.reshape(steps, count, ht, 2, HD).transpose(1, 2, 3, 0, 4)
    fresh = jnp.pad(fresh, ((0, 0), (0, 0), (0, 0), (0, rows - steps), (0, 0)))
    small = jnp.concatenate([asked, fresh], axis=2)
    V, D = pltpu.VMEM, pltpu.SemaphoreType.DMA
    smem = pl.BlockSpec(memory_space=pltpu.SMEM)
    anywhere = pl.BlockSpec(memory_space=pl.ANY)
    vmem = pl.BlockSpec(memory_space=pltpu.VMEM)
    result = pl.pallas_call(
        functools.partial(kernel, R, T),
        out_shape=jax.ShapeDtypeStruct((R, ht, rows, HD), bf16),
        in_specs=[smem, smem, smem, anywhere, anywhere, vmem],
        out_specs=vmem,
        scratch_shapes=[
            V((tokens, features), bf16),
            V((2, heads, features, HD), bf16),
            V((heads + 1, tokens, HD), bf16),
            V((R, ht, 3, rows, HD), bf16),
            V((heads, R, rows, HD), bf16),
            V((8, 128), i32),
            V((R, 8, 128), i32),
            V((rows, tokens), i32),
            V((heads, rows, tokens), f32),
            V((T, ht, rows, tokens), f32),
            V((heads, rows, tokens), bf16),
            V((ht, R, rows, HD), f32),
            V((heads, R * rows, HD), f32),
            V((T, ht, R * rows, HD), f32),
            V((R, ht, rows, HD), bf16),
            V((R, ht, rows, HD), bf16),
            D(()), D((2, 2)), D((R,)), D((R,)), D((R,)), D((R,)), D((T,)), D((T,)),
            D((2, R, 2, CHUNKS)), D((2, R, CHUNKS)), D((2, R, CHUNKS)), D((2, R, CHUNKS)),
            D((heads,)), D((T, ht)), D((T,)), D((T,)), D((heads,)), D((T, ht)), D((R,)), D((R,)),
        ],
        compiler_params=pltpu.CompilerParams(
            collective_id=0, has_side_effects=True, vmem_limit_bytes=48 * 1024 * 1024
        ),
        cost_estimate=pl.CostEstimate(
            flops=2 * tokens * features * heads * 2 * HD,
            bytes_accessed=2 * (tokens * features + features * heads * HD),
            transcendentals=0,
        ),
    )(owners, pages, lengths, prompts, kv_weight, small)
    result = result.reshape(R, ht, steps, GQA, HD).transpose(2, 0, 1, 3, 4)
    return result.reshape(steps, R, width)


def solution(mesh):
    R, T = mesh.shape["req"], mesh.shape["tp"]

    def on_device(prompts, kv_weight, owners, pages, lengths, queries, new_kv):
        whole_heads = (
            mesh.shape["parts"] == 2
            and kv_weight.shape[1] == 4 * HD
            and queries.shape[2] * T == 2 * R * GQA * HD
            and queries.shape[0] == 2
            and R > 1
        )
        body = functools.partial(fused, R, T) if whole_heads else general
        return body(prompts, kv_weight, owners, pages, lengths, queries, new_kv)

    return jax.shard_map(
        on_device,
        mesh=mesh,
        in_specs=(
            P(("parts", "req"), "tp"),
            P("tp", "req"),
            P(("parts", "req"), None),
            P(("parts", "req"), None),
            P(("parts", "req"), None),
            P(None, ("parts", "req"), "tp"),
            P(None, ("parts", "req"), "tp"),
        ),
        out_specs=P(None, ("parts", "req"), "tp"),
        check_vma=False,
    )
```

```python
import functools

import jax
import jax.numpy as jnp
from jax import lax
from jax.experimental import pallas as pl
from jax.experimental.pallas import tpu as pltpu
from jax.sharding import PartitionSpec as P

HD = 128
PAGE = 16
GQA = 8
CHUNKS = 4
TILE = 256
MESH = pl.DeviceIdType.MESH
SCALE = HD ** (-0.5)


def attend(queries, new_kv, cache, row_lengths):
    steps_count, rows_count = (queries.shape[0], queries.shape[1])
    heads_kv = new_kv.shape[2] // (2 * HD)
    slot_tokens = cache.shape[1]
    score_scale = HD ** (-0.5)
    asked = queries.reshape(steps_count, rows_count, heads_kv, GQA, HD)
    fresh = new_kv.reshape(steps_count, rows_count, heads_kv, 2, HD)
    stored = cache.reshape(rows_count, slot_tokens, heads_kv, 2, HD)
    cached = (
        jnp.einsum(
            "srhgd,rthd->srhgt", asked, stored[:, :, :, 0], preferred_element_type=jnp.float32
        )
        * score_scale
    )
    newer = (
        jnp.einsum(
            "srhgd,urhd->srhgu", asked, fresh[:, :, :, 0], preferred_element_type=jnp.float32
        )
        * score_scale
    )
    valid = jnp.arange(slot_tokens, dtype=jnp.int32)[None, :] < row_lengths[:, None]
    seen = jnp.arange(steps_count)[None, :] <= jnp.arange(steps_count)[:, None]
    cached = jnp.where(valid[None, :, None, None, :], cached, -1e30)
    newer = jnp.where(seen[:, None, None, None, :], newer, -1e30)
    top = jnp.maximum(jnp.max(cached, axis=-1), jnp.max(newer, axis=-1))[..., None]
    weight_cached = jnp.exp(cached - top)
    weight_newer = jnp.exp(newer - top)
    total = jnp.sum(weight_cached, axis=-1, keepdims=True) + jnp.sum(
        weight_newer, axis=-1, keepdims=True
    )
    prob_cached = (weight_cached / total).astype(jnp.bfloat16)
    prob_newer = (weight_newer / total).astype(jnp.bfloat16)
    mixed = jnp.einsum(
        "srhgt,rthd->srhgd", prob_cached, stored[:, :, :, 1], preferred_element_type=jnp.float32
    )
    mixed = mixed + jnp.einsum(
        "srhgu,urhd->srhgd", prob_newer, fresh[:, :, :, 1], preferred_element_type=jnp.float32
    )
    return mixed.astype(jnp.bfloat16).reshape(steps_count, rows_count, heads_kv * GQA * HD)


def general(prompts, kv_weight, owners, pages, lengths, queries, new_kv):
    owner_count = lax.axis_size("req")
    tokens_here = prompts.shape[0]
    group_pages = tokens_here // PAGE
    most_pages = 5 * group_pages // (2 * owner_count)
    slot_tokens = most_pages * PAGE
    partial_value = jnp.dot(
        prompts,
        lax.all_gather(kv_weight, "req", axis=1, tiled=True),
        preferred_element_type=jnp.float32,
    )
    key_value = lax.psum_scatter(
        partial_value.astype(jnp.bfloat16), "tp", scatter_dimension=1, tiled=True
    )
    width_here = key_value.shape[1]
    padded = jnp.concatenate(
        [key_value, jnp.zeros((slot_tokens, width_here), jnp.bfloat16)], axis=0
    )
    starts = jnp.cumsum(pages[0]) - pages[0]
    chosen_mask = (owners[0][None, :] == jnp.arange(owner_count, dtype=jnp.int32)[:, None]).astype(
        jnp.int32
    )
    target_starts = jnp.sum(chosen_mask * starts[None, :], axis=1) * PAGE
    outgoing = jax.vmap(lambda offset: lax.dynamic_slice_in_dim(padded, offset, slot_tokens, 0))(
        target_starts
    )
    incoming = lax.all_to_all(outgoing, "req", split_axis=0, concat_axis=0, tiled=True)
    return attend(queries, new_kv, incoming, lengths[0])


def kernel(
    R, T, owners_hbm, pages_hbm, lengths_hbm, x_hbm, w_hbm, q_hbm, n_hbm, out,
    owners, pages, lengths, q_in, n_in, small, x, w, kvb, msg, qall, lens_out, lens_in, tok, s_part, s_recv, p_all, fresh_o,
    o_part, o_recv, o_send, fin,
    in_sem, x_sem, w_sem, msg_s, msg_r, len_s, len_r, q_s, q_r,
    z_s, z_r, y_s, y_r, s_s, s_r, p_s, p_r, o_s, o_r, f_s, f_r,
):
    p, r, t = lax.axis_index("parts"), lax.axis_index("req"), lax.axis_index("tp")
    tokens = x.shape[0]
    features = w.shape[2]
    part_rows = features // CHUNKS
    ht = small.shape[1]
    heads = R * 2
    rows = small.shape[3]
    f32 = jnp.float32

    def when(cond):
        return pl.when(cond)

    x_copy = pltpu.make_async_copy(x_hbm, x, x_sem)
    own = [
        pltpu.make_async_copy(
            w_hbm.at[:, pl.ds((2 * i + kv) * HD, HD)], w.at[kv, 2 * r + i], w_sem.at[kv, i]
        )
        for kv in range(2)
        for i in range(2)
    ]
    inputs = [
        pltpu.make_async_copy(a, b, in_sem.at[n])
        for n, (a, b) in enumerate(
            [(q_hbm, q_in), (n_hbm, n_in), (owners_hbm, owners), (pages_hbm, pages), (lengths_hbm, lengths)]
        )
    ]
    for copy in own[:2] + inputs + own[2:]:
        copy.start()
    x_copy.start()

    barrier = pltpu.get_barrier_semaphore()
    for rel in range(1, R):
        pl.semaphore_signal(barrier, inc=1, device_id={"req": lax.rem(r + rel, R)}, device_id_type=MESH)
    for rel in range(1, T):
        pl.semaphore_signal(barrier, inc=1, device_id={"tp": lax.rem(t + rel, T)}, device_id_type=MESH)
    pl.semaphore_signal(barrier, inc=1, device_id={"parts": 1 - p}, device_id_type=MESH)

    for copy in own[:2]:
        copy.wait()
    pl.semaphore_wait(barrier, R + T - 1)

    def remote(src, dst, s, d, where):
        return pltpu.make_async_remote_copy(
            src_ref=src, dst_ref=dst, send_sem=s, recv_sem=d, device_id=where, device_id_type=MESH
        )

    def msg_copy(rel):
        to = lax.rem(r + rel, R)
        return remote(small.at[to], msg.at[r], msg_s.at[rel], msg_r.at[rel], {"req": to})

    def msg_arrival(rel):
        of = lax.rem(r + R - rel, R)
        return remote(small.at[of], msg.at[of], msg_s.at[rel], msg_r.at[rel], {"req": of})

    def len_copy(rel):
        to = lax.rem(r + rel, R)
        return remote(lens_out, lens_in.at[r], len_s.at[rel], len_r.at[rel], {"req": to})

    def len_arrival(rel):
        of = lax.rem(r + R - rel, R)
        return remote(lens_out, lens_in.at[of], len_s.at[rel], len_r.at[rel], {"req": of})

    def piece(kv, h, c):
        return w.at[kv, h, pl.ds(pl.multiple_of(c * part_rows, part_rows), part_rows)]

    def z_copy(kv, s, c, direction):
        to = r - 1 if direction == 0 else r + 1
        ref = piece(kv, 2 * s + p, c)
        return remote(ref, ref, z_s.at[kv, s, direction, c], z_r.at[kv, s, c], {"req": to})

    def y_copy(kv, s, c):
        ref = piece(kv, 2 * s + p, c)
        return remote(ref, ref, y_s.at[kv, s, c], y_r.at[kv, s, c], {"parts": 1 - p})

    def y_arrival(kv, s, c):
        ref = piece(kv, 2 * s + 1 - p, c)
        return remote(ref, ref, y_s.at[kv, s, c], y_r.at[kv, s, c], {"parts": 1 - p})

    def z_arrival(kv, s, c, direction):
        ref = piece(kv, 2 * s + p, c)
        of = r + 1 if direction == 0 else r - 1
        return remote(ref, ref, z_s.at[kv, s, direction, c], z_r.at[kv, s, c], {"req": of})

    can = (r > 0, r < R - 1)

    def send_own(kv):
        for c in range(CHUNKS):
            for direction in range(2):
                @when(can[direction])
                def _():
                    z_copy(kv, r, c, direction).start()

    send_own(0)
    for copy in own[2:]:
        copy.wait()
    send_own(1)

    for copy in inputs:
        copy.wait()
    lane = lax.broadcasted_iota(jnp.int32, (8, 128), 1)
    row_len = jnp.zeros((8, 128), jnp.int32)
    for g in range(R):
        row_len = jnp.where(lane == g, lengths[0, g], row_len)
    lens_out[...] = row_len
    lens_in[r] = row_len
    steps = q_in.shape[0]
    asked = [q_in[s].astype(f32) for s in range(steps)]
    newer = [n_in[s].astype(f32) for s in range(steps)]
    nothing = jnp.zeros((rows - steps, HD), f32)
    for g in range(R):
        for i in range(ht):
            small[g, i, 0] = jnp.concatenate(
                [
                    asked[s][g:g + 1, (i * GQA + j) * HD:(i * GQA + j + 1) * HD]
                    for s in range(steps)
                    for j in range(GQA)
                ],
                axis=0,
            ).astype(jnp.bfloat16)
            for kv in range(2):
                at = (2 * i + kv) * HD
                small[g, i, 1 + kv] = jnp.concatenate(
                    [newer[s][g:g + 1, at:at + HD] for s in range(steps)] + [nothing], axis=0
                ).astype(jnp.bfloat16)
    for rel in range(1, R):
        msg_copy(rel).start()
        len_copy(rel).start()
    msg[r] = small[r]

    for rel in range(1, R):
        msg_arrival(rel).wait_recv()
        len_arrival(rel).wait_recv()
    for i in range(ht):
        for o in range(R):
            qall[t * ht + i, o] = msg[o, i, 0]

    def q_copy(rel):
        ref = qall.at[pl.ds(t * ht, ht)]
        return remote(ref, ref, q_s.at[rel], q_r.at[rel], {"tp": lax.rem(t + rel, T)})

    def q_arrival(rel):
        of = lax.rem(t + T - rel, T)
        ref = qall.at[pl.ds(of * ht, ht)]
        return remote(ref, ref, q_s.at[rel], q_r.at[rel], {"tp": of})

    for rel in range(1, T):
        q_copy(rel).start()

    position = lax.broadcasted_iota(jnp.int32, (rows, tokens), 1)
    owner_of = jnp.full((rows, tokens), -1, jnp.int32)
    for o in range(R):
        begin = jnp.int32(0)
        running = jnp.int32(0)
        for j in range(R):
            begin = begin + jnp.where(owners[0, j] == o, running, 0)
            running = running + pages[0, j] * PAGE
        length = jnp.sum(jnp.where(lane[:1] == r, lens_in[o][:1], 0), axis=1, keepdims=True)
        inside = (position >= begin) & (position < begin + length)
        owner_of = jnp.where(inside, o, owner_of)
    tok[...] = owner_of

    def s_copy(h):
        to, i = h // ht, lax.rem(h, ht)
        return remote(s_part.at[h], s_recv.at[t, i], s_s.at[h], s_r.at[t, i], {"tp": to})

    def o_copy(h):
        to, i = h // ht, lax.rem(h, ht)
        return remote(o_part.at[h], o_recv.at[t, i], o_s.at[h], o_r.at[t, i], {"tp": to})

    def process(kv, h):
        slot = jnp.where(kv == 1, h, heads)

        def tile(n, carry):
            at = pl.ds(pl.multiple_of(n * TILE, TILE), TILE)
            kvb[slot, at, :] = jnp.dot(
                x[at, :], w[kv, h], preferred_element_type=f32
            ).astype(jnp.bfloat16)
            return carry

        lax.fori_loop(0, tokens // TILE, tile, 0)

        @when(kv == 0)
        def _():
            scores = lax.dot_general(
                qall[h].reshape(R * rows, HD), kvb[heads],
                (((1,), (1,)), ((), ())), preferred_element_type=f32,
            )
            belongs = tok[...]
            chosen = jnp.zeros((rows, tokens), f32)
            for o in range(R):
                chosen = jnp.where(belongs == o, scores[o * rows:(o + 1) * rows], chosen)
            s_part[h] = chosen

            @when(h // ht != t)
            def _():
                s_copy(h).start()

    def others(n):
        return [lax.rem(t + rel, n) for rel in range(1, n)]

    def p_copy(rel):
        ref = p_all.at[pl.ds(t * ht, ht)]
        return remote(ref, ref, p_s.at[rel], p_r.at[rel], {"tp": lax.rem(t + rel, T)})

    def p_arrival(rel):
        of = lax.rem(t + T - rel, T)
        ref = p_all.at[pl.ds(of * ht, ht)]
        return remote(ref, ref, p_s.at[rel], p_r.at[rel], {"tp": of})

    def softmax():
        belongs = tok[...]
        row = lax.broadcasted_iota(jnp.int32, (rows, rows), 0)
        col = lax.broadcasted_iota(jnp.int32, (rows, rows), 1)
        seen = col * GQA <= row
        for i in range(ht):
            h = t * ht + i
            total = s_part[h]
            for of in others(T):
                remote(s_part.at[h], s_recv.at[of, i], s_s.at[h], s_r.at[of, i], {"tp": of}).wait_recv()
                total = total + s_recv[of, i]
            total = total * SCALE
            probs = jnp.zeros((rows, tokens), f32)
            for o in range(R):
                newer = lax.dot_general(
                    msg[o, i, 0], msg[o, i, 1], (((1,), (1,)), ((), ())),
                    preferred_element_type=f32,
                ) * SCALE
                newer = jnp.where(seen, newer, -1e30)
                mine = jnp.where(belongs == o, total, -1e30)
                top = jnp.maximum(
                    jnp.max(mine, axis=1, keepdims=True), jnp.max(newer, axis=1, keepdims=True)
                )
                e_old = jnp.exp(mine - top)
                e_new = jnp.exp(newer - top)
                den = jnp.sum(e_old, axis=1, keepdims=True) + jnp.sum(e_new, axis=1, keepdims=True)
                probs = jnp.where(belongs == o, e_old / den, probs)
                fresh_o[i, o] = jnp.dot(
                    (e_new / den).astype(jnp.bfloat16), msg[o, i, 2], preferred_element_type=f32
                )
            p_all[h] = probs.astype(jnp.bfloat16)
        for rel in range(1, T):
            p_copy(rel).start()

    hops = R - 1
    last = 2 * hops

    def source(step, side):
        kv, d = step // hops, lax.rem(step, hops) + 1
        s = r + d if side == 0 else r - d
        valid = s < R if side == 0 else s >= 0
        return kv, s, valid

    def forward(step, c):
        for side in range(2):
            kv, s, valid = source(step, side)

            @when(valid)
            def _():
                z_arrival(kv, s, c, side).wait_recv()

                @when(can[side])
                def _():
                    z_copy(kv, s, c, side).start()

                y_copy(kv, s, c).start()

    def mix(h):
        belongs = tok[...]
        probs = p_all[h].astype(f32)
        split = jnp.concatenate(
            [jnp.where(belongs == o, probs, 0.0).astype(jnp.bfloat16) for o in range(R)], axis=0
        )
        o_part[h] = jnp.dot(split, kvb[h], preferred_element_type=f32)

        @when(h // ht != t)
        def _():
            o_copy(h).start()

    def piece_of(step, j):
        late, side = j // 2, lax.rem(j, 2)
        at = jnp.maximum(step - 1, 0)
        kv, d = at // hops, lax.rem(at, hops) + 1
        s = jnp.where(side == 0, r + d, r - d)
        first = step == 0
        valid = first | ((s < R) & (s >= 0))
        h = jnp.where(first, 2 * r + side, 2 * s + jnp.where(late == 1, 1 - p, p))
        return jnp.where(first, 1 - late, kv), s, h, valid, (late == 1) & (step > 0)

    def work(step, j):
        kv, s, h, valid, across = piece_of(step, j)

        @when(valid & across)
        def _():
            for c in range(CHUNKS):
                y_arrival(kv, s, c).wait_recv()

        @when(valid)
        def _():
            process(kv, h)

        return h, valid

    def step_body(step, carry):
        def slot(j, carry):
            @when(step < last)
            def _():
                forward(step, j)

            @when((step == 0) & (j == 0))
            def _():
                x_copy.wait()

            @when((step == 0) & (j == 2))
            def _():
                for rel in range(1, T):
                    q_arrival(rel).wait_recv()

            h, valid = work(step, j)

            @when((step == last) & valid)
            def _():
                mix(h)

            return carry

        lax.fori_loop(0, 4, slot, 0)

        @when(step == R)
        def _():
            softmax()

        @when(step == last - 1)
        def _():
            for rel in range(1, T):
                p_arrival(rel).wait_recv()

            def early(n, carry):
                s = n // 2
                away = jnp.where(s > r, s - r, r - s)

                @when(away < hops)
                def _():
                    mix(n)

                return carry

            lax.fori_loop(0, heads, early, 0)

        return carry

    lax.fori_loop(0, last + 1, step_body, 0)

    for i in range(ht):
        h = t * ht + i
        total = o_part[h]
        for of in others(T):
            remote(o_part.at[h], o_recv.at[of, i], o_s.at[h], o_r.at[of, i], {"tp": of}).wait_recv()
            total = total + o_recv[of, i]
        for o in range(R):
            o_send[o, i] = (total[o * rows:(o + 1) * rows] + fresh_o[i, o]).astype(jnp.bfloat16)

    def f_copy(rel):
        to = lax.rem(r + rel, R)
        return remote(o_send.at[to], fin.at[r], f_s.at[rel], f_r.at[rel], {"req": to})

    def f_arrival(rel):
        of = lax.rem(r + R - rel, R)
        return remote(o_send.at[of], fin.at[of], f_s.at[rel], f_r.at[rel], {"req": of})

    for rel in range(1, R):
        f_copy(rel).start()
    fin[r] = o_send[r]

    for rel in range(1, R):
        msg_copy(rel).wait_send()
        len_copy(rel).wait_send()
    for rel in range(1, T):
        q_copy(rel).wait_send()
        p_copy(rel).wait_send()
    for kv in range(2):
        for s in range(R):
            for c in range(CHUNKS):
                @when((s >= r) & can[0])
                def _():
                    z_copy(kv, s, c, 0).wait_send()

                @when((s <= r) & can[1])
                def _():
                    z_copy(kv, s, c, 1).wait_send()

                @when(s != r)
                def _():
                    y_copy(kv, s, c).wait_send()
    for h in range(heads):
        @when(h // ht != t)
        def _():
            s_copy(h).wait_send()
            o_copy(h).wait_send()
    for rel in range(1, R):
        f_copy(rel).wait_send()
        f_arrival(rel).wait_recv()
    got = [[fin[g, i].astype(f32) for i in range(ht)] for g in range(R)]
    for s in range(steps):
        out[s] = jnp.concatenate(
            [
                jnp.concatenate(
                    [got[g][i][s * GQA + j:s * GQA + j + 1] for i in range(ht) for j in range(GQA)], axis=1
                )
                for g in range(R)
            ],
            axis=0,
        ).astype(jnp.bfloat16)


def fused(R, T, prompts, kv_weight, owners, pages, lengths, queries, new_kv):
    steps, count, width = queries.shape
    ht = width // (GQA * HD)
    heads = 2 * R
    rows = steps * GQA
    tokens, features = prompts.shape
    bf16, f32, i32 = jnp.bfloat16, jnp.float32, jnp.int32
    V, D = pltpu.VMEM, pltpu.SemaphoreType.DMA
    anywhere = pl.BlockSpec(memory_space=pl.ANY)
    vmem = pl.BlockSpec(memory_space=pltpu.VMEM)
    return pl.pallas_call(
        functools.partial(kernel, R, T),
        out_shape=jax.ShapeDtypeStruct((steps, R, width), bf16),
        in_specs=[anywhere] * 7,
        out_specs=vmem,
        scratch_shapes=[
            pltpu.SMEM(owners.shape, i32), pltpu.SMEM(pages.shape, i32), pltpu.SMEM(lengths.shape, i32),
            V(queries.shape, bf16),
            V(new_kv.shape, bf16),
            V((R, ht, 3, rows, HD), bf16),
            V((tokens, features), bf16),
            V((2, heads, features, HD), bf16),
            V((heads + 1, tokens, HD), bf16),
            V((R, ht, 3, rows, HD), bf16),
            V((heads, R, rows, HD), bf16),
            V((8, 128), i32),
            V((R, 8, 128), i32),
            V((rows, tokens), i32),
            V((heads, rows, tokens), f32),
            V((T, ht, rows, tokens), f32),
            V((heads, rows, tokens), bf16),
            V((ht, R, rows, HD), f32),
            V((heads, R * rows, HD), f32),
            V((T, ht, R * rows, HD), f32),
            V((R, ht, rows, HD), bf16),
            V((R, ht, rows, HD), bf16),
            D((5,)), D(()), D((2, 2)), D((R,)), D((R,)), D((R,)), D((R,)), D((T,)), D((T,)),
            D((2, R, 2, CHUNKS)), D((2, R, CHUNKS)), D((2, R, CHUNKS)), D((2, R, CHUNKS)),
            D((heads,)), D((T, ht)), D((T,)), D((T,)), D((heads,)), D((T, ht)), D((R,)), D((R,)),
        ],
        compiler_params=pltpu.CompilerParams(
            collective_id=0, has_side_effects=True, vmem_limit_bytes=48 * 1024 * 1024
        ),
        cost_estimate=pl.CostEstimate(
            flops=2 * tokens * features * heads * 2 * HD,
            bytes_accessed=2 * (tokens * features + features * heads * HD),
            transcendentals=0,
        ),
    )(owners, pages, lengths, prompts, kv_weight, queries, new_kv)


def solution(mesh):
    R, T = mesh.shape["req"], mesh.shape["tp"]

    def on_device(prompts, kv_weight, owners, pages, lengths, queries, new_kv):
        whole_heads = (
            mesh.shape["parts"] == 2
            and kv_weight.shape[1] == 4 * HD
            and queries.shape[2] * T == 2 * R * GQA * HD
            and queries.shape[0] == 2
            and R > 2
        )
        body = functools.partial(fused, R, T) if whole_heads else general
        return body(prompts, kv_weight, owners, pages, lengths, queries, new_kv)

    return jax.shard_map(
        on_device,
        mesh=mesh,
        in_specs=(
            P(("parts", "req"), "tp"),
            P("tp", "req"),
            P(("parts", "req"), None),
            P(("parts", "req"), None),
            P(("parts", "req"), None),
            P(None, ("parts", "req"), "tp"),
            P(None, ("parts", "req"), "tp"),
        ),
        out_specs=P(None, ("parts", "req"), "tp"),
        check_vma=False,
    )
```
